512 devices in a mesh: replica: 16 (over y, z_lo), fsdp: 32 (over x, z_hi, core).
Axes of the slice: x: 4, y: 8, z: 8 (z_hi: 4, z_lo: 2; z = z_hi * 2 + z_lo), core: 2. Of those that a mesh axis runs over, the one named last changes fastest.
Arguments:
- tokens: bfloat16 [16, 16384, 2048], P('replica', 'fsdp'), may hold values from -6 to 6
- key_cot: bfloat16 [16, 16384, 512], P('replica', 'fsdp'), may hold values from -6 to 6
- norm_gain: float32 [2048], replicated, may hold values from 0.25 to 1.75
- key_weight: float32 [16, 2048, 512], P('replica', 'fsdp'), may hold values from -0.125 to 0.125
- first_moment: float32 [16, 2048, 512], P('replica', 'fsdp'), may hold values from -60 to 60
- second_moment: float32 [16, 2048, 512], P('replica', 'fsdp'), may hold values from 10 to 1000
- inner_step: int32 [1], replicated, may hold values from 1 to 8
- global_prev: float32 [2048, 512], P('fsdp'), may hold values from -6 to 6
- outer_momentum: float32 [2048, 512], P('fsdp'), may hold values from -6 to 6
- replica_prev: float32 [16, 2048, 512], P('replica', 'fsdp'), may hold values from -6 to 6
Outputs:
- weight_new: float32 [16, 2048, 512], P('replica', 'fsdp')
- first_new: float32 [16, 2048, 512], P('replica', 'fsdp')
- second_new: float32 [16, 2048, 512], P('replica', 'fsdp')
- keys: bfloat16 [16, 16384, 512], P('replica', 'fsdp')
- blended: float32 [16, 2048, 512], P('replica', 'fsdp')
- momentum_new: float32 [2048, 512], P('fsdp')
The draws below stay inside these ranges and needn't reach their ends.
Inputs may be any that keep to these rules, and one draw needn't show every extreme that they name: `inner_step`: the inner optimizer's step count, the same for every replica.
All inputs are finite; a program needn't handle non-finite values.
Results may differ from the reference program's by a relative error of at most 0.025.
Values may be sent and summed in bfloat16 or wider, within the bound.
A program may use at most 64 MiB of HBM per device.

```python
import math
import jax
import jax.numpy as jnp
from jax import lax

D = 2048
KW = 512
TOK_DEV = 512
TOK_REP = 16384
REPLICAS = 16
N_REPLICA = 16
N_FSDP = 32


def with_spikes(array, key, source, target, blocks, factor):
    def block_of(axis_at):
        return (jnp.arange(array.shape[axis_at]) // (array.shape[axis_at] // blocks)).reshape((-1,) + (1,) * (array.ndim - 1 - axis_at))

    first = jax.random.permutation(key, blocks)[block_of(target)]
    other_side = (block_of(target) + blocks // 2) % blocks
    return jnp.where((block_of(source) == first) | (block_of(source) == other_side), factor * array, array)


def level_of(own_key, shape, shards, low, top_value):
    def one(axis_at, parts):
        steps = jax.random.uniform(jax.random.fold_in(jax.random.fold_in(own_key, 6), axis_at), (parts,), jnp.float32, low / len(shards), top_value / len(shards))
        return jnp.repeat(jnp.exp(steps), shape[axis_at] // parts).reshape((-1,) + (1,) * (len(shape) - axis_at - 1))

    factor_of = one(*shards[0])
    for cut in shards[1:]:
        factor_of = factor_of * one(*cut)
    return factor_of


def normal_values(own_key, extent, scale, limit, shards=(), held_as=jnp.bfloat16):
    gain = level_of(own_key, extent, shards, -0.22, 0.18) if shards else 1.0
    drawn = jax.random.normal(own_key, extent, jnp.float32) * scale * gain
    return jnp.minimum(jnp.maximum(drawn, -limit), limit).astype(held_as)


def noise_with(key, extent, spread, limit, cuts, heavy, kind=jnp.bfloat16):
    values = spread * jax.random.normal(key, extent, jnp.float32)
    if cuts:
        values = values * level_of(key, extent, cuts, -0.22, 0.18)
    return jnp.clip(with_spikes(values, jax.random.fold_in(key, 3), *heavy), -limit, limit).astype(kind)


def setup_inputs(seed: int = 0) -> dict:
    key_of = jax.random.split(jax.random.key(seed), 11)
    return {
        "tokens": noise_with(key_of[0], (REPLICAS, TOK_REP, D), 1.0, 6.0, ((0, 16), (1, 32)), (1, 2, 32, 2.75)),
        "key_cot": normal_values(key_of[1], (REPLICAS, TOK_REP, KW), 1.0, 6.0, ((0, 16), (1, 32))),
        "norm_gain": jnp.clip(1.0 + 0.15 * jax.random.normal(key_of[2], (D,), jnp.float32), 0.25, 1.75),
        "key_weight": normal_values(key_of[3], (REPLICAS, D, KW), D ** -0.5, 0.125, ((0, 16), (1, 32)), jnp.float32),
        "first_moment": normal_values(key_of[4], (REPLICAS, D, KW), 10.0, 60.0, ((0, 16), (1, 32)), jnp.float32),
        "second_moment": jnp.clip(jnp.exp(math.log(1000.0) - 4.6051702 * jax.random.uniform(key_of[5], (REPLICAS, D, KW), jnp.float32) ** level_of(key_of[5], (REPLICAS, D, KW), ((0, 16), (1, 32)), -0.2, 0.2)), 10.0, 1000.0),
        "inner_step": jax.random.randint(key_of[6], (1,), 1, 9).astype(jnp.int32),
        "global_prev": normal_values(key_of[7], (D, KW), 1.0, 6.0, ((0, 32),), jnp.float32),
        "outer_momentum": normal_values(key_of[8], (D, KW), 1.0, 6.0, ((0, 32),), jnp.float32),
        "replica_prev": normal_values(key_of[9], (REPLICAS, D, KW), 1.0, 6.0, ((0, 16), (1, 32)), jnp.float32),
    }


def rms_normed(tokens, norm_gain):
    values = tokens.astype(jnp.float32)
    scale = lax.rsqrt(lax.optimization_barrier(jnp.mean(values * values, axis=-1, keepdims=True)) + 1e-05)
    return (values * scale * norm_gain).astype(jnp.bfloat16)

def adam_step(weight, first, second, grads, inner_step):
    count = inner_step[0].astype(jnp.float32)
    first_new = 0.9 * first + 0.1 * grads
    second_new = 0.95 * second + 0.05 * grads * grads
    first_hat = first_new / (1.0 - jnp.power(jnp.float32(0.9), count))
    second_hat = second_new / (1.0 - jnp.power(jnp.float32(0.95), count))
    change = 0.03 * (first_hat / (jnp.sqrt(second_hat) + 1e-08) + 0.1 * weight)
    return (change, first_new, second_new)

def replica_grads(pair):
    normed, cotangent = pair
    normed_blocks = normed.reshape(N_FSDP, TOK_DEV, D)
    cot_blocks = cotangent.reshape(N_FSDP, TOK_DEV, KW)

    def add_block(total, block):
        term = lax.dot_general(block[0], block[1], (((0,), (0,)), ((), ())), preferred_element_type=jnp.float32)
        rounded = lax.optimization_barrier(term.astype(jnp.bfloat16))
        return (total + rounded.astype(jnp.float32), None)
    total, unused = lax.scan(add_block, jnp.zeros((D, KW), jnp.float32), (normed_blocks, cot_blocks))
    return total

def replica_keys(pair):
    normed, weight = pair
    return jnp.dot(normed, weight.astype(jnp.bfloat16), preferred_element_type=jnp.float32).astype(jnp.bfloat16)

def reference(tokens, key_cot, norm_gain, key_weight, first_moment, second_moment, inner_step, global_prev, outer_momentum, replica_prev):
    normed = rms_normed(tokens, norm_gain)
    grads = lax.map(replica_grads, (normed, key_cot))
    change, first_new, second_new = adam_step(key_weight, first_moment, second_moment, grads, inner_step)
    weight_new = key_weight - change
    keys = lax.map(replica_keys, (normed, weight_new))
    mean_drift = lax.optimization_barrier(jnp.sum(global_prev[None] - replica_prev, axis=0)) / N_REPLICA
    momentum_new = 0.9 * outer_momentum + mean_drift
    global_new = global_prev - 0.7 * (mean_drift + 0.9 * momentum_new)
    blended = 0.5 * global_new[None] + 0.5 * replica_prev
    return (weight_new, first_new, second_new, keys, blended, momentum_new)
```

```python
import math

import jax
import jax.numpy as jnp
from jax import lax
from jax.experimental import pallas as pl
from jax.experimental.pallas import tpu as pltpu
from jax.sharding import PartitionSpec as P

F32, BF16 = jnp.float32, jnp.bfloat16
MESH = pl.DeviceIdType.MESH
TOK, D, KW, ROWS, WIDE = 512, 2048, 512, 64, 256
CONTRACT_FIRST = (((0,), (0,)), ((), ()))

CHUNKS = (
    (1, 32, 16, "z", 0),
    (1, 48, 16, "z", 1),
    (1, 0, 16, "x", 0),
    (1, 16, 16, "x", 1),
    (0, 0, 32, "x", 0),
    (0, 32, 32, "x", 1),
)
HALVES = (1, 0)
N_SEMS = 17


def pair_bit(kind, p):
    return ((p + 1) // 2) % 2 if kind == 0 else p // 2


def pair_of(kind, p):
    return p + 1 - 2 * (p % 2) if kind == 0 else 3 - p


class Place:
    def __init__(self):
        f, r = lax.axis_index("fsdp"), lax.axis_index("replica")
        self.x, self.z, self.c = f // 8, (f // 2) % 4, f % 2
        self.y, self.l = r // 2, r % 2

    def at(self, **other):
        v = {**vars(self), **other}
        return (v["y"] * 2 + v["l"], (v["x"] * 4 + v["z"]) * 2 + v["c"])

    def partners(self):
        for o in (1, 2, 3):
            yield self.at(x=(self.x + o) % 4)
            yield self.at(z=(self.z + o) % 4)
        yield self.at(c=1 - self.c)
        for step in range(4):
            yield self.drift_partner(step)

    def drift_partner(self, step):
        y = self.y
        if step == 0:
            return self.at(y=y + 1 - 2 * (y % 2))
        if step == 1:
            return self.at(y=y + 2 - 4 * ((y // 2) % 2))
        if step == 2:
            return self.at(y=(y + 4) % 8)
        return self.at(l=1 - self.l)


def up(ref_value):
    return ref_value.astype(F32)


def chunk_steps(here, chunk, bufs, sems, w_ref, adam):
    half, row0, nr, axis, first = chunk
    g, rc, s1, r1, s2, r2, sq, rq = bufs
    send_sem, recv_sem = sems
    other_axis = "z" if axis == "x" else "x"
    p, q, c = getattr(here, axis), getattr(here, other_axis), here.c
    k1, k2 = first, 1 - first
    b1, b2 = pair_bit(k1, p), pair_bit(k2, p)
    p1, p2 = pair_of(k1, p), pair_of(k2, p)
    to1, to2 = here.at(**{axis: p1}), here.at(**{axis: p2})
    sibling = here.at(c=1 - c)
    started = []

    def copy(n, src, dst, to):
        return pltpu.make_async_remote_copy(
            src_ref=src,
            dst_ref=dst,
            send_sem=send_sem.at[n],
            recv_sem=recv_sem.at[n],
            device_id=to,
            device_id_type=MESH,
        )

    def send(*what):
        one = copy(*what)
        one.start()
        started.append(one)
        return one

    def drain(keep):
        while len(started) > keep:
            started.pop(0).wait_send()

    c_out = send(0, g.at[1 - c, 1 - b1], rc.at[1 - b1], sibling)
    c_in = send(1, g.at[1 - c, b1], rc.at[b1], sibling)
    yield
    c_out.wait_recv()
    for part, n in ((1 - b2, 2), (b2, 3)):
        s1[part] = (up(g[c, 1 - b1, part]) + up(rc[1 - b1, part])).astype(BF16)
        if n == 2:
            first_in = send(2, s1.at[part], r1.at[part], to1)
        else:
            second_in = send(3, s1.at[part], r1.at[part], to1)
    yield
    c_in.wait_recv()
    first_in.wait_recv()
    s2[...] = (up(g[c, b1, 1 - b2]) + up(rc[b1, 1 - b2]) + up(r1[1 - b2])).astype(BF16)
    pair_in = send(4, s2, r2, to2)
    yield
    second_in.wait_recv()
    drain(1)
    pair_in.wait_recv()
    sq[...] = (up(g[c, b1, b2]) + up(rc[b1, b2]) + up(r1[b2]) + up(r2[...])).astype(BF16)
    direct = []
    for o in (2, 1, 3):
        to = (q + o) % 4
        direct.append(send(4 + o, sq.at[to], rq.at[o - 1], here.at(**{other_axis: to})))
    yield
    drain(3)
    for one in direct:
        one.wait_recv()
    total = up(sq[q]) + up(rq[0]) + up(rq[1]) + up(rq[2])
    w_own = adam(half, row0, nr, total)

    def piece(pp, qq, cc):
        x, z = (pp, qq) if axis == "x" else (qq, pp)
        return w_ref.at[half, x, z, cc, pl.ds(row0, nr)]

    def group(pp, cc):
        if axis == "x":
            return w_ref.at[half, pp, :, cc, pl.ds(row0, nr)]
        return w_ref.at[half, :, pp, cc, pl.ds(row0, nr)]

    mine = piece(p, q, c)
    mine[...] = w_own
    direct = []
    for o in (2, 1, 3):
        direct.append(send(7 + o, mine, mine, here.at(**{other_axis: (q + o) % 4})))
    yield
    drain(3)
    for one in direct:
        one.wait_recv()
    own = group(p, c)
    in2 = send(11, own, own, to2)
    in1 = send(12, own, own, to1)
    cs = [send(13, own, own, sibling)]
    yield
    drain(3)
    in2.wait_recv()
    own = group(p2, c)
    in12 = send(14, own, own, to1)
    cs.append(send(15, own, own, sibling))
    yield
    drain(2)
    in1.wait_recv()
    own = group(p1, c)
    cs.append(send(16, own, own, sibling))
    yield
    in12.wait_recv()
    own = group(pair_of(k2, p1), c)
    cs.append(send(17, own, own, sibling))
    yield
    for one in cs:
        one.wait_recv()
    yield
    drain(0)
    yield


def kernel(
    tokens, key_cot, gain, key_weight, first_moment, second_moment, inner_step, global_prev, outer_momentum, replica_prev,
    weight_out, first_out, second_out, keys_out, blended_out, momentum_out,
    tok, cot, cs, scale, kw, m1, m2, gp, om, rp, gcol, wn, fn, sn, bl, mn, keys, w_all, ds, dr,
    in_sem, out_sem, d_send, d_recv, *chunk_scratch,
):
    here = Place()
    c = here.c

    def load(src, dst, n):
        one = pltpu.make_async_copy(src, dst, in_sem.at[n])
        one.start()
        return one

    quarter = TOK // 4
    tok_in = [load(tokens.at[0, pl.ds(i * quarter, quarter)], tok.at[pl.ds(i * quarter, quarter)], i) for i in range(4)]
    cot_in = load(key_cot.at[0], cot, 4)
    rest = [
        load(key_weight.at[0], kw, 5),
        load(first_moment.at[0], m1, 6),
        load(second_moment.at[0], m2, 7),
        load(global_prev, gp, 8),
        load(outer_momentum, om, 9),
    ]
    rp_in = load(replica_prev.at[0], rp, 10)

    barrier = pltpu.get_barrier_semaphore()
    n_partners = 0
    for to in here.partners():
        pl.semaphore_signal(barrier, inc=1, device_id=to, device_id_type=MESH)
        n_partners += 1

    for i in range(4):
        tok_in[i].wait()
        if i == 0:
            cot_in.wait()
        rows = slice(i * quarter, (i + 1) * quarter)
        v = up(tok[rows, :])
        s = lax.rsqrt(jnp.sum(v * v, axis=1, keepdims=True) * (1.0 / D) + 1e-05)
        scale[rows, :] = s
        cs[rows, :] = (up(cot[rows, :]) * s).astype(BF16)

    def gemm1(half):
        for x in range(4):
            part = lax.dot_general(
                tok[:, x * 512 : (x + 1) * 512],
                cs[:, half * WIDE : (half + 1) * WIDE],
                CONTRACT_FIRST,
                preferred_element_type=F32,
            ).astype(BF16)
            for i, (h, row0, nr, axis, first) in enumerate(CHUNKS):
                if h != half:
                    continue
                g = chunk_scratch[10 * i]
                for z in range(4):
                    p, q = (x, z) if axis == "x" else (z, x)
                    b1, b2 = pair_bit(first, p), pair_bit(1 - first, p)
                    for cc in range(2):
                        at = (z * 2 + cc) * ROWS + row0
                        g[cc, b1, b2, q] = part[at : at + nr]

    def adam(half, row0, nr, total):
        rows, cols = slice(row0, row0 + nr), slice(half * WIDE, (half + 1) * WIDE)
        count = jnp.full((1, WIDE), inner_step[0], jnp.int32).astype(F32)
        gains = gcol[rows, :]
        grads = total * gains
        first_new = 0.9 * m1[rows, cols] + 0.1 * grads
        second_new = 0.95 * m2[rows, cols] + 0.05 * grads * grads
        first_hat = first_new / (1.0 - jnp.exp(count * math.log(0.9)))
        second_hat = second_new / (1.0 - jnp.exp(count * math.log(0.95)))
        weight = kw[rows, cols]
        change = 0.03 * (first_hat / (jnp.sqrt(second_hat) + 1e-08) + 0.1 * weight)
        weight_new = weight - change
        fn[rows, cols] = first_new
        sn[rows, cols] = second_new
        wn[rows, cols] = weight_new
        return (weight_new * gains).astype(BF16)

    outs = []

    def store(src, dst):
        one = pltpu.make_async_copy(src, dst, out_sem.at[len(outs)])
        one.start()
        outs.append(one)

    def drift_steps():
        rp_in.wait()
        ds[0] = rp[...].astype(BF16)
        for step in range(4):
            one = pltpu.make_async_remote_copy(
                src_ref=ds.at[step],
                dst_ref=dr.at[step],
                send_sem=d_send.at[step],
                recv_sem=d_recv.at[step],
                device_id=here.drift_partner(step),
                device_id_type=MESH,
            )
            one.start()
            yield
            one.wait()
            total = up(ds[step]) + up(dr[step])
            if step < 3:
                ds[step + 1] = total.astype(BF16)
        mean_drift = gp[...] - total * (1.0 / 16)
        momentum_new = 0.9 * om[...] + mean_drift
        global_new = gp[...] - 0.7 * (mean_drift + 0.9 * momentum_new)
        mn[...] = momentum_new
        bl[...] = 0.5 * global_new + 0.5 * rp[...]
        store(mn, momentum_out)
        store(bl, blended_out.at[0])
        yield

    def gemm2(half):
        w = w_all[half].reshape(D, WIDE)
        cols = slice(half * WIDE, (half + 1) * WIDE)
        part = jnp.dot(tok[...], w, preferred_element_type=F32)
        keys[half] = (part * scale[...]).astype(BF16)
        store(keys.at[half], keys_out.at[0, :, pl.ds(half * WIDE, WIDE)])

    chunks = [
        chunk_steps(here, chunk, chunk_scratch[10 * i : 10 * i + 8], chunk_scratch[10 * i + 8 : 10 * i + 10], w_all, adam)
        for i, chunk in enumerate(CHUNKS)
    ]
    drift = drift_steps()

    gemm1(HALVES[0])
    pl.semaphore_wait(barrier, n_partners)
    for i, chunk in enumerate(CHUNKS):
        if chunk[0] == HALVES[0]:
            next(chunks[i])
    next(drift)
    gemm1(HALVES[1])
    for i, chunk in enumerate(CHUNKS):
        if chunk[0] == HALVES[1]:
            next(chunks[i])
    for one in rest:
        one.wait()
    lane = lax.broadcasted_iota(jnp.int32, (ROWS, 128), 1)
    row = lax.broadcasted_iota(jnp.int32, (ROWS, 128), 0)
    gains = gain[pl.ds(here.x * 4 + here.z, 1), :]
    picked = jnp.where(lane == row + ROWS * c, jnp.broadcast_to(gains, (ROWS, 128)), 0.0)
    gcol[...] = jnp.broadcast_to(jnp.sum(picked, axis=1, keepdims=True), (ROWS, WIDE))

    for level in range(1, 9):
        for one in chunks:
            next(one)
        if level == 4:
            store(wn, weight_out.at[0])
            store(fn, first_out.at[0])
            store(sn, second_out.at[0])
        if 2 <= level <= 5:
            next(drift)
    for half in HALVES:
        for i, chunk in enumerate(CHUNKS):
            if chunk[0] == half:
                next(chunks[i])
        gemm2(half)
    for one in chunks:
        next(one)
    for one in outs:
        one.wait()


def chunk_scratch(nr):
    return [
        pltpu.VMEM((2, 2, 2, 4, nr, WIDE), BF16),
        pltpu.VMEM((2, 2, 4, nr, WIDE), BF16),
        pltpu.VMEM((2, 4, nr, WIDE), BF16),
        pltpu.VMEM((2, 4, nr, WIDE), BF16),
        pltpu.VMEM((4, nr, WIDE), BF16),
        pltpu.VMEM((4, nr, WIDE), BF16),
        pltpu.VMEM((4, nr, WIDE), BF16),
        pltpu.VMEM((3, nr, WIDE), BF16),
        pltpu.SemaphoreType.DMA((18,)),
        pltpu.SemaphoreType.DMA((18,)),
    ]


def body(tokens, key_cot, norm_gain, key_weight, first_moment, second_moment, inner_step, global_prev, outer_momentum, replica_prev):
    anywhere = pl.BlockSpec(memory_space=pl.ANY)
    small = jax.ShapeDtypeStruct((1, ROWS, KW), F32)
    shard = pltpu.VMEM((ROWS, KW), F32)
    scratch = [
        pltpu.VMEM((TOK, D), BF16),
        pltpu.VMEM((TOK, KW), BF16),
        pltpu.VMEM((TOK, KW), BF16),
        pltpu.VMEM((TOK, 1), F32),
        *[shard] * 6,
        pltpu.VMEM((ROWS, WIDE), F32),
        *[shard] * 5,
        pltpu.VMEM((2, TOK, WIDE), BF16),
        pltpu.VMEM((2, 4, 4, 2, ROWS, WIDE), BF16),
        pltpu.VMEM((4, ROWS, KW), BF16),
        pltpu.VMEM((4, ROWS, KW), BF16),
        pltpu.SemaphoreType.DMA((11,)),
        pltpu.SemaphoreType.DMA((7,)),
        pltpu.SemaphoreType.DMA((4,)),
        pltpu.SemaphoreType.DMA((4,)),
    ]
    for chunk in CHUNKS:
        scratch += chunk_scratch(chunk[2])
    return pl.pallas_call(
        kernel,
        out_shape=(
            small,
            small,
            small,
            jax.ShapeDtypeStruct((1, TOK, KW), BF16),
            small,
            jax.ShapeDtypeStruct((ROWS, KW), F32),
        ),
        in_specs=[
            anywhere,
            anywhere,
            pl.BlockSpec(memory_space=pltpu.VMEM),
            anywhere,
            anywhere,
            anywhere,
            pl.BlockSpec(memory_space=pltpu.SMEM),
            anywhere,
            anywhere,
            anywhere,
        ],
        out_specs=(anywhere,) * 6,
        scratch_shapes=scratch,
        name="step",
        compiler_params=pltpu.CompilerParams(
            collective_id=0, has_side_effects=True, vmem_limit_bytes=56 * 2**20
        ),
    )(
        tokens, key_cot, norm_gain.reshape(16, 128), key_weight, first_moment, second_moment, inner_step,
        global_prev, outer_momentum, replica_prev,
    )


def solution(mesh):
    split = P("replica", "fsdp", None)
    rows = P("fsdp", None)
    return jax.shard_map(
        body,
        mesh=mesh,
        in_specs=(split, split, P(), split, split, split, P(), rows, rows, split),
        out_specs=(split, split, split, split, split, rows),
        check_vma=False,
    )
```

```python
import math

import jax
import jax.numpy as jnp
from jax import lax
from jax.experimental import pallas as pl
from jax.experimental.pallas import tpu as pltpu
from jax.sharding import PartitionSpec as P

F32, BF16 = jnp.float32, jnp.bfloat16
MESH = pl.DeviceIdType.MESH
TOK, D, KW, ROWS, WIDE = 512, 2048, 512, 64, 256
CONTRACT_FIRST = (((0,), (0,)), ((), ()))

CHUNKS = (
    (1, 32, 32, "z"),
    (1, 0, 32, "x"),
    (0, 0, 32, "x"),
    (0, 32, 32, "x"),
)
HALVES = (1, 0)
OFFSETS = (2, 1, 3)


class Place:
    def __init__(self):
        f, r = lax.axis_index("fsdp"), lax.axis_index("replica")
        self.x, self.z, self.c = f // 8, (f // 2) % 4, f % 2
        self.y, self.l = r // 2, r % 2

    def at(self, **other):
        v = {**vars(self), **other}
        return (v["y"] * 2 + v["l"], (v["x"] * 4 + v["z"]) * 2 + v["c"])

    def partners(self):
        for o in OFFSETS:
            yield self.at(z=(self.z + o) % 4)
        for o in OFFSETS:
            yield self.at(x=(self.x + o) % 4)
        yield self.at(c=1 - self.c)
        yield self.at(l=1 - self.l)
        yield self.at(y=(self.y + 1) % 8)
        yield self.at(y=(self.y + 7) % 8)


def up(ref_value):
    return ref_value.astype(F32)


def remote(src, dst, send_sem, recv_sem, to):
    return pltpu.make_async_remote_copy(
        src_ref=src,
        dst_ref=dst,
        send_sem=send_sem,
        recv_sem=recv_sem,
        device_id=to,
        device_id_type=MESH,
    )


def chunk_steps(here, chunk, bufs, sems, w_ref, adam):
    half, row0, nr, axis = chunk
    g, rc, s1, r1, sq, rq = bufs
    send_sem, recv_sem = sems
    other_axis = "z" if axis == "x" else "x"
    p, q, c = getattr(here, axis), getattr(here, other_axis), here.c
    sibling = here.at(c=1 - c)

    def along_p(o):
        return here.at(**{axis: (p + o) % 4})

    def along_q(o):
        return here.at(**{other_axis: (q + o) % 4})

    def send(n, src, dst, to, m=None):
        one = remote(src, dst, send_sem.at[n], recv_sem.at[n if m is None else m], to)
        one.start()
        return one

    def all_of(n, ref):
        return remote(ref, ref, send_sem.at[n], recv_sem.at[n], sibling)

    swap = send(0, g.at[1 - c], rc, sibling)
    yield
    swap.wait_recv()
    for o in OFFSETS:
        to = (p + o) % 4
        s1[to] = (up(g[c, to]) + up(rc[to])).astype(BF16)
        send(1, s1.at[to], r1.at[o - 1], along_p(o))
    yield
    mine = up(g[c, p]) + up(rc[p])
    all_of(1, r1).wait_recv()
    sq[...] = (mine + up(r1[0]) + up(r1[1]) + up(r1[2])).astype(BF16)
    for o in OFFSETS:
        send(2, sq.at[(q + o) % 4], rq.at[o - 1], along_q(o))
    yield
    swap.wait_send()
    all_of(2, rq).wait_recv()
    w_own = adam(half, row0, nr, up(sq[q]) + up(rq[0]) + up(rq[1]) + up(rq[2]))

    def piece(pp, qq, cc):
        x, z = (pp, qq) if axis == "x" else (qq, pp)
        return w_ref.at[half, x, z, cc, pl.ds(row0, nr)]

    def group(pp, cc):
        if axis == "x":
            return w_ref.at[half, pp, :, cc, pl.ds(row0, nr)]
        return w_ref.at[half, :, pp, cc, pl.ds(row0, nr)]

    own = piece(p, q, c)
    own[...] = w_own
    for o in OFFSETS:
        send(3, own, own, along_q(o))
    yield
    all_of(1, r1).wait_send()
    all_of(3, rq).wait_recv()
    own = group(p, c)
    come = [send(4, own, own, along_p(o), 4 + o) for o in OFFSETS]
    send(8, own, own, sibling)
    yield
    all_of(2, rq).wait_send()
    all_of(3, rq).wait_send()
    for i, o in ((1, 1), (2, 3), (0, 2)):
        come[i].wait_recv()
        got = group((p + 4 - o) % 4, c)
        send(8, got, got, sibling)
    yield
    all_of(4, r1).wait_send()
    all_of(8, s1).wait()
    yield


def kernel(
    tokens, key_cot, gain, key_weight, first_moment, second_moment, inner_step, global_prev, outer_momentum, replica_prev,
    weight_out, first_out, second_out, keys_out, blended_out, momentum_out,
    tok, cot, cs, scale, kw, m1, m2, gp, om, rp, gcol, wn, fn, sn, bl, mn, keys, w_all, ds, dy,
    step_smem, in_sem, out_sem, d_send, d_recv, *chunk_scratch,
):
    here = Place()
    c = here.c

    barrier = pltpu.get_barrier_semaphore()
    n_partners = 0
    for to in here.partners():
        pl.semaphore_signal(barrier, inc=1, device_id=to, device_id_type=MESH)
        n_partners += 1

    def load(src, dst, n):
        one = pltpu.make_async_copy(src, dst, in_sem.at[n])
        one.start()
        return one

    quarter = TOK // 4
    tok_in = [load(tokens.at[0, pl.ds(i * quarter, quarter)], tok.at[pl.ds(i * quarter, quarter)], i) for i in range(4)]
    cot_in = load(key_cot.at[0], cot, 4)
    rest = [
        load(key_weight.at[0], kw, 5),
        load(first_moment.at[0], m1, 6),
        load(second_moment.at[0], m2, 7),
        load(global_prev, gp, 8),
        load(outer_momentum, om, 9),
        load(inner_step, step_smem, 11),
    ]
    rp_in = load(replica_prev.at[0], rp, 10)

    for i in range(4):
        tok_in[i].wait()
        if i == 0:
            cot_in.wait()
        rows = slice(i * quarter, (i + 1) * quarter)
        v = up(tok[rows, :])
        s = lax.rsqrt(jnp.sum(v * v, axis=1, keepdims=True) * (1.0 / D) + 1e-05)
        scale[rows, :] = s
        cs[rows, :] = (up(cot[rows, :]) * s).astype(BF16)

    def gemm1(half):
        for x in range(4):
            part = lax.dot_general(
                tok[:, x * 512 : (x + 1) * 512],
                cs[:, half * WIDE : (half + 1) * WIDE],
                CONTRACT_FIRST,
                preferred_element_type=F32,
            ).astype(BF16)
            for i, (h, row0, nr, axis) in enumerate(CHUNKS):
                if h != half:
                    continue
                g = chunk_scratch[8 * i]
                for z in range(4):
                    p, q = (x, z) if axis == "x" else (z, x)
                    for cc in range(2):
                        at = (z * 2 + cc) * ROWS + row0
                        g[cc, p, q] = part[at : at + nr]

    def adam(half, row0, nr, total):
        rows, cols = slice(row0, row0 + nr), slice(half * WIDE, (half + 1) * WIDE)
        count = jnp.full((1, WIDE), step_smem[0], jnp.int32).astype(F32)
        gains = gcol[rows, :]
        grads = total * gains
        first_new = 0.9 * m1[rows, cols] + 0.1 * grads
        second_new = 0.95 * m2[rows, cols] + 0.05 * grads * grads
        first_hat = first_new / (1.0 - jnp.exp(count * math.log(0.9)))
        second_hat = second_new / (1.0 - jnp.exp(count * math.log(0.95)))
        weight = kw[rows, cols]
        change = 0.03 * (first_hat / (jnp.sqrt(second_hat) + 1e-08) + 0.1 * weight)
        weight_new = weight - change
        fn[rows, cols] = first_new
        sn[rows, cols] = second_new
        wn[rows, cols] = weight_new
        return (weight_new * gains).astype(BF16)

    outs = []

    def store(src, dst):
        one = pltpu.make_async_copy(src, dst, out_sem.at[len(outs)])
        one.start()
        outs.append(one)

    def drift_steps():
        y = here.y
        rp_in.wait()
        ds[0] = rp[...].astype(BF16)
        swap = remote(ds.at[0], ds.at[1], d_send.at[0], d_recv.at[0], here.at(l=1 - here.l))
        swap.start()
        yield
        swap.wait()
        dy[y] = (up(ds[0]) + up(ds[1])).astype(BF16)
        went = []
        for k in range(4):
            come = []
            for n, step in ((1 + k, 1), (5 + k, 7)):
                if k == 3 and step == 7:
                    continue
                slot = dy.at[(y + (8 - step) * k) % 8]
                one = remote(slot, slot, d_send.at[n], d_recv.at[n], here.at(y=(y + step) % 8))
                one.start()
                come.append(one)
            went += come
            yield
            for one in come:
                one.wait_recv()
        total = up(dy[0])
        for i in range(1, 8):
            total = total + up(dy[i])
        mean_drift = gp[...] - total * (1.0 / 16)
        momentum_new = 0.9 * om[...] + mean_drift
        global_new = gp[...] - 0.7 * (mean_drift + 0.9 * momentum_new)
        mn[...] = momentum_new
        bl[...] = 0.5 * global_new + 0.5 * rp[...]
        store(mn, momentum_out)
        store(bl, blended_out.at[0])
        for one in went:
            one.wait_send()
        yield

    def gemm2(half):
        w = w_all[half].reshape(D, WIDE)
        cols = slice(half * WIDE, (half + 1) * WIDE)
        part = jnp.dot(tok[...], w, preferred_element_type=F32)
        keys[half] = (part * scale[...]).astype(BF16)
        store(keys.at[half], keys_out.at[0, :, pl.ds(half * WIDE, WIDE)])

    chunks = [
        chunk_steps(here, chunk, chunk_scratch[8 * i : 8 * i + 6], chunk_scratch[8 * i + 6 : 8 * i + 8], w_all, adam)
        for i, chunk in enumerate(CHUNKS)
    ]
    drift = drift_steps()

    gemm1(HALVES[0])
    pl.semaphore_wait(barrier, n_partners)
    for i, chunk in enumerate(CHUNKS):
        if chunk[0] == HALVES[0]:
            next(chunks[i])
    next(drift)
    gemm1(HALVES[1])
    for i, chunk in enumerate(CHUNKS):
        if chunk[0] == HALVES[1]:
            next(chunks[i])
    for one in rest:
        one.wait()
    lane = lax.broadcasted_iota(jnp.int32, (ROWS, 128), 1)
    row = lax.broadcasted_iota(jnp.int32, (ROWS, 128), 0)
    gains = gain[pl.ds(here.x * 4 + here.z, 1), :]
    picked = jnp.where(lane == row + ROWS * c, jnp.broadcast_to(gains, (ROWS, 128)), 0.0)
    gcol[...] = jnp.broadcast_to(jnp.sum(picked, axis=1, keepdims=True), (ROWS, WIDE))

    for level in range(1, 6):
        for one in chunks:
            next(one)
        if level == 3:
            store(wn, weight_out.at[0])
            store(fn, first_out.at[0])
            store(sn, second_out.at[0])
        next(drift)
    for half in HALVES:
        for i, chunk in enumerate(CHUNKS):
            if chunk[0] == half:
                next(chunks[i])
        gemm2(half)
    for one in outs:
        one.wait()


def chunk_scratch(nr):
    return [
        pltpu.VMEM((2, 4, 4, nr, WIDE), BF16),
        pltpu.VMEM((4, 4, nr, WIDE), BF16),
        pltpu.VMEM((4, 4, nr, WIDE), BF16),
        pltpu.VMEM((3, 4, nr, WIDE), BF16),
        pltpu.VMEM((4, nr, WIDE), BF16),
        pltpu.VMEM((3, nr, WIDE), BF16),
        pltpu.SemaphoreType.DMA((9,)),
        pltpu.SemaphoreType.DMA((9,)),
    ]


def hand_over(*refs):
    given, wanted, held, sems = refs[:6], refs[6:12], refs[12:18], refs[18]
    come = [pltpu.make_async_copy(given[i], held[i], sems.at[0, i]) for i in range(6)]
    go = [pltpu.make_async_copy(held[i], wanted[i], sems.at[1, i]) for i in range(6)]
    for one in come:
        one.start()
    for i in range(6):
        come[i].wait()
        go[i].start()
    for one in go:
        one.wait()


def body(tokens, key_cot, norm_gain, key_weight, first_moment, second_moment, inner_step, global_prev, outer_momentum, replica_prev):
    anywhere = pl.BlockSpec(memory_space=pl.ANY)
    small = jax.ShapeDtypeStruct((1, ROWS, KW), F32)
    shard = pltpu.VMEM((ROWS, KW), F32)
    scratch = [
        pltpu.VMEM((TOK, D), BF16),
        pltpu.VMEM((TOK, KW), BF16),
        pltpu.VMEM((TOK, KW), BF16),
        pltpu.VMEM((TOK, 1), F32),
        *[shard] * 6,
        pltpu.VMEM((ROWS, WIDE), F32),
        *[shard] * 5,
        pltpu.VMEM((2, TOK, WIDE), BF16),
        pltpu.VMEM((2, 4, 4, 2, ROWS, WIDE), BF16),
        pltpu.VMEM((2, ROWS, KW), BF16),
        pltpu.VMEM((8, ROWS, KW), BF16),
        pltpu.SMEM((1,), jnp.int32),
        pltpu.SemaphoreType.DMA((12,)),
        pltpu.SemaphoreType.DMA((7,)),
        pltpu.SemaphoreType.DMA((8,)),
        pltpu.SemaphoreType.DMA((8,)),
    ]
    for chunk in CHUNKS:
        scratch += chunk_scratch(chunk[2])
    results = pl.pallas_call(
        kernel,
        out_shape=(
            small,
            small,
            small,
            jax.ShapeDtypeStruct((1, TOK, KW), BF16),
            small,
            jax.ShapeDtypeStruct((ROWS, KW), F32),
        ),
        in_specs=[
            anywhere,
            anywhere,
            pl.BlockSpec(memory_space=pltpu.VMEM),
            anywhere,
            anywhere,
            anywhere,
            anywhere,
            anywhere,
            anywhere,
            anywhere,
        ],
        out_specs=(anywhere,) * 6,
        scratch_shapes=scratch,
        name="step",
        compiler_params=pltpu.CompilerParams(
            collective_id=0, has_side_effects=True, vmem_limit_bytes=56 * 2**20
        ),
    )(
        tokens, key_cot, norm_gain.reshape(16, 128), key_weight, first_moment, second_moment, inner_step,
        global_prev, outer_momentum, replica_prev,
    )
    return pl.pallas_call(
        hand_over,
        out_shape=tuple(jax.ShapeDtypeStruct(a.shape, a.dtype) for a in results),
        in_specs=[anywhere] * 6,
        out_specs=(anywhere,) * 6,
        scratch_shapes=[*[pltpu.VMEM(a.shape, a.dtype) for a in results], pltpu.SemaphoreType.DMA((2, 6))],
        name="hand_over",
    )(*results)


def solution(mesh):
    split = P("replica", "fsdp", None)
    rows = P("fsdp", None)
    return jax.shard_map(
        body,
        mesh=mesh,
        in_specs=(split, split, P(), split, split, split, P(), rows, rows, split),
        out_specs=(split, split, split, split, split, rows),
        check_vma=False,
    )
```

```python
import math

import jax
import jax.numpy as jnp
from jax import lax
from jax.experimental import pallas as pl
from jax.experimental.pallas import tpu as pltpu
from jax.sharding import PartitionSpec as P

F32, BF16 = jnp.float32, jnp.bfloat16
MESH = pl.DeviceIdType.MESH
TOK, D, KW, ROWS, WIDE = 512, 2048, 512, 64, 256
CONTRACT_FIRST = (((0,), (0,)), ((), ()))

CHUNKS = ((1, 32, 16, 'z'), (1, 0, 16, 'x'), (1, 48, 16, 'z'), (1, 16, 16, 'x'), (0, 0, 16, 'x'), (0, 16, 16, 'x'), (0, 32, 16, 'x'), (0, 48, 16, 'x'))
HALVES = (1, 0)
OFFSETS = (2, 1, 3)


class Place:
    def __init__(self):
        f, r = lax.axis_index("fsdp"), lax.axis_index("replica")
        self.x, self.z, self.c = f // 8, (f // 2) % 4, f % 2
        self.y, self.l = r // 2, r % 2

    def at(self, **other):
        v = {**vars(self), **other}
        return (v["y"] * 2 + v["l"], (v["x"] * 4 + v["z"]) * 2 + v["c"])

    def partners(self):
        for o in OFFSETS:
            yield self.at(z=(self.z + o) % 4)
        for o in OFFSETS:
            yield self.at(x=(self.x + o) % 4)
        yield self.at(c=1 - self.c)
        yield self.at(l=1 - self.l)
        yield self.at(y=(self.y + 1) % 8)
        yield self.at(y=(self.y + 7) % 8)


def up(ref_value):
    return ref_value.astype(F32)


def remote(src, dst, send_sem, recv_sem, to):
    return pltpu.make_async_remote_copy(
        src_ref=src,
        dst_ref=dst,
        send_sem=send_sem,
        recv_sem=recv_sem,
        device_id=to,
        device_id_type=MESH,
    )


def chunk_steps(here, chunk, bufs, sems, w_ref, adam):
    half, row0, nr, axis = chunk
    g, rc, s1, r1, sq, rq = bufs
    send_sem, recv_sem = sems
    other_axis = "z" if axis == "x" else "x"
    p, q, c = getattr(here, axis), getattr(here, other_axis), here.c
    sibling = here.at(c=1 - c)

    def along_p(o):
        return here.at(**{axis: (p + o) % 4})

    def along_q(o):
        return here.at(**{other_axis: (q + o) % 4})

    def send(n, src, dst, to, m=None):
        one = remote(src, dst, send_sem.at[n], recv_sem.at[n if m is None else m], to)
        one.start()
        return one

    def all_of(n, ref):
        return remote(ref, ref, send_sem.at[n], recv_sem.at[n], sibling)

    swap = send(0, g.at[1 - c], rc, sibling)
    yield
    swap.wait_recv()
    for o in OFFSETS:
        to = (p + o) % 4
        s1[to] = (up(g[c, to]) + up(rc[to])).astype(BF16)
        send(1, s1.at[to], r1.at[o - 1], along_p(o))
    yield
    mine = up(g[c, p]) + up(rc[p])
    all_of(1, r1).wait_recv()
    sq[...] = (mine + up(r1[0]) + up(r1[1]) + up(r1[2])).astype(BF16)
    for o in OFFSETS:
        send(2, sq.at[(q + o) % 4], rq.at[o - 1], along_q(o))
    yield
    swap.wait_send()
    all_of(2, rq).wait_recv()
    w_own = adam(half, row0, nr, up(sq[q]) + up(rq[0]) + up(rq[1]) + up(rq[2]))

    def piece(pp, qq, cc):
        x, z = (pp, qq) if axis == "x" else (qq, pp)
        return w_ref.at[half, x, z, cc, pl.ds(row0, nr)]

    def group(pp, cc):
        if axis == "x":
            return w_ref.at[half, pp, :, cc, pl.ds(row0, nr)]
        return w_ref.at[half, :, pp, cc, pl.ds(row0, nr)]

    own = piece(p, q, c)
    own[...] = w_own
    for o in OFFSETS:
        send(3, own, own, along_q(o))
    yield
    all_of(1, r1).wait_send()
    all_of(3, rq).wait_recv()
    own = group(p, c)
    come = [send(4, own, own, along_p(o), 4 + o) for o in OFFSETS]
    send(8, own, own, sibling)
    yield
    all_of(2, rq).wait_send()
    all_of(3, rq).wait_send()
    for i, o in ((1, 1), (2, 3), (0, 2)):
        come[i].wait_recv()
        got = group((p + 4 - o) % 4, c)
        send(8, got, got, sibling)
    yield
    all_of(4, r1).wait_send()
    all_of(8, s1).wait()
    yield


def kernel(
    tokens, key_cot, gain, key_weight, first_moment, second_moment, inner_step, global_prev, outer_momentum, replica_prev,
    weight_out, first_out, second_out, keys_out, blended_out, momentum_out,
    tok, cot, cs, scale, kw, m1, m2, gp, om, rp, gcol, w_all, ds, dy,
    step_smem, in_sem, d_send, d_recv, *chunk_scratch,
):
    here = Place()
    c = here.c

    barrier = pltpu.get_barrier_semaphore()
    n_partners = 0
    for to in here.partners():
        pl.semaphore_signal(barrier, inc=1, device_id=to, device_id_type=MESH)
        n_partners += 1

    def load(src, dst, n):
        one = pltpu.make_async_copy(src, dst, in_sem.at[n])
        one.start()
        return one

    quarter = TOK // 4
    tok_in = [load(tokens.at[0, pl.ds(i * quarter, quarter)], tok.at[pl.ds(i * quarter, quarter)], i) for i in range(4)]
    cot_in = load(key_cot.at[0], cot, 4)
    rest = [
        load(key_weight.at[0], kw, 5),
        load(first_moment.at[0], m1, 6),
        load(second_moment.at[0], m2, 7),
        load(global_prev, gp, 8),
        load(outer_momentum, om, 9),
        load(inner_step, step_smem, 11),
    ]
    rp_in = load(replica_prev.at[0], rp, 10)

    for i in range(4):
        tok_in[i].wait()
        if i == 0:
            cot_in.wait()
        rows = slice(i * quarter, (i + 1) * quarter)
        v = up(tok[rows, :])
        s = lax.rsqrt(jnp.sum(v * v, axis=1, keepdims=True) * (1.0 / D) + 1e-05)
        scale[rows, :] = s
        cs[rows, :] = (up(cot[rows, :]) * s).astype(BF16)

    def gemm1(half):
        for x in range(4):
            part = lax.dot_general(
                tok[:, x * 512 : (x + 1) * 512],
                cs[:, half * WIDE : (half + 1) * WIDE],
                CONTRACT_FIRST,
                preferred_element_type=F32,
            ).astype(BF16)
            for i, (h, row0, nr, axis) in enumerate(CHUNKS):
                if h != half:
                    continue
                g = chunk_scratch[8 * i]
                for z in range(4):
                    p, q = (x, z) if axis == "x" else (z, x)
                    for cc in range(2):
                        at = (z * 2 + cc) * ROWS + row0
                        g[cc, p, q] = part[at : at + nr]

    def adam(half, row0, nr, total):
        rows, cols = slice(row0, row0 + nr), slice(half * WIDE, (half + 1) * WIDE)
        count = jnp.full((1, WIDE), step_smem[0], jnp.int32).astype(F32)
        gains = gcol[rows, :]
        grads = total * gains
        first_new = 0.9 * m1[rows, cols] + 0.1 * grads
        second_new = 0.95 * m2[rows, cols] + 0.05 * grads * grads
        first_hat = first_new / (1.0 - jnp.exp(count * math.log(0.9)))
        second_hat = second_new / (1.0 - jnp.exp(count * math.log(0.95)))
        weight = kw[rows, cols]
        change = 0.03 * (first_hat / (jnp.sqrt(second_hat) + 1e-08) + 0.1 * weight)
        weight_new = weight - change
        first_out[0, rows, cols] = first_new
        second_out[0, rows, cols] = second_new
        weight_out[0, rows, cols] = weight_new
        return (weight_new * gains).astype(BF16)

    def drift_steps():
        y = here.y
        rp_in.wait()
        ds[0] = rp[...].astype(BF16)
        swap = remote(ds.at[0], ds.at[1], d_send.at[0], d_recv.at[0], here.at(l=1 - here.l))
        swap.start()
        yield
        swap.wait()
        dy[y] = (up(ds[0]) + up(ds[1])).astype(BF16)
        went = []
        for k in range(4):
            come = []
            for n, step in ((1 + k, 1), (5 + k, 7)):
                if k == 3 and step == 7:
                    continue
                slot = dy.at[(y + (8 - step) * k) % 8]
                one = remote(slot, slot, d_send.at[n], d_recv.at[n], here.at(y=(y + step) % 8))
                one.start()
                come.append(one)
            went += come
            yield
            for one in come:
                one.wait_recv()
        total = up(dy[0])
        for i in range(1, 8):
            total = total + up(dy[i])
        mean_drift = gp[...] - total * (1.0 / 16)
        momentum_new = 0.9 * om[...] + mean_drift
        global_new = gp[...] - 0.7 * (mean_drift + 0.9 * momentum_new)
        momentum_out[...] = momentum_new
        blended_out[0] = 0.5 * global_new + 0.5 * rp[...]
        for one in went:
            one.wait_send()
        yield

    def gemm2(half):
        w = w_all[half].reshape(D, WIDE)
        cols = slice(half * WIDE, (half + 1) * WIDE)
        part = jnp.dot(tok[...], w, preferred_element_type=F32)
        keys_out[0, :, cols] = (part * scale[...]).astype(BF16)

    chunks = [
        chunk_steps(here, chunk, chunk_scratch[8 * i : 8 * i + 6], chunk_scratch[8 * i + 6 : 8 * i + 8], w_all, adam)
        for i, chunk in enumerate(CHUNKS)
    ]
    drift = drift_steps()

    gemm1(HALVES[0])
    pl.semaphore_wait(barrier, n_partners)
    for i, chunk in enumerate(CHUNKS):
        if chunk[0] == HALVES[0]:
            next(chunks[i])
    next(drift)
    gemm1(HALVES[1])
    for i, chunk in enumerate(CHUNKS):
        if chunk[0] == HALVES[1]:
            next(chunks[i])
    for one in rest:
        one.wait()
    lane = lax.broadcasted_iota(jnp.int32, (ROWS, 128), 1)
    row = lax.broadcasted_iota(jnp.int32, (ROWS, 128), 0)
    gains = gain[pl.ds(here.x * 4 + here.z, 1), :]
    picked = jnp.where(lane == row + ROWS * c, jnp.broadcast_to(gains, (ROWS, 128)), 0.0)
    gcol[...] = jnp.broadcast_to(jnp.sum(picked, axis=1, keepdims=True), (ROWS, WIDE))

    for level in range(1, 6):
        for one in chunks:
            next(one)
        next(drift)
    for half in HALVES:
        for i, chunk in enumerate(CHUNKS):
            if chunk[0] == half:
                next(chunks[i])
        gemm2(half)


def chunk_scratch(nr):
    return [
        pltpu.VMEM((2, 4, 4, nr, WIDE), BF16),
        pltpu.VMEM((4, 4, nr, WIDE), BF16),
        pltpu.VMEM((4, 4, nr, WIDE), BF16),
        pltpu.VMEM((3, 4, nr, WIDE), BF16),
        pltpu.VMEM((4, nr, WIDE), BF16),
        pltpu.VMEM((3, nr, WIDE), BF16),
        pltpu.SemaphoreType.DMA((9,)),
        pltpu.SemaphoreType.DMA((9,)),
    ]


def hand_over(*refs):
    sems = refs[12]
    copies = [pltpu.make_async_copy(refs[i], refs[6 + i], sems.at[i]) for i in range(6)]
    for one in copies:
        one.start()
    for one in copies:
        one.wait()


def body(tokens, key_cot, norm_gain, key_weight, first_moment, second_moment, inner_step, global_prev, outer_momentum, replica_prev):
    anywhere = pl.BlockSpec(memory_space=pl.ANY)
    in_hbm = pl.BlockSpec(memory_space=pltpu.HBM)
    small = pltpu.VMEM((1, ROWS, KW), F32)
    shard = pltpu.VMEM((ROWS, KW), F32)
    scratch = [
        pltpu.VMEM((TOK, D), BF16),
        pltpu.VMEM((TOK, KW), BF16),
        pltpu.VMEM((TOK, KW), BF16),
        pltpu.VMEM((TOK, 1), F32),
        *[shard] * 6,
        pltpu.VMEM((ROWS, WIDE), F32),
        pltpu.VMEM((2, 4, 4, 2, ROWS, WIDE), BF16),
        pltpu.VMEM((2, ROWS, KW), BF16),
        pltpu.VMEM((8, ROWS, KW), BF16),
        pltpu.SMEM((1,), jnp.int32),
        pltpu.SemaphoreType.DMA((12,)),
        pltpu.SemaphoreType.DMA((8,)),
        pltpu.SemaphoreType.DMA((8,)),
    ]
    for chunk in CHUNKS:
        scratch += chunk_scratch(chunk[2])
    results = pl.pallas_call(
        kernel,
        out_shape=(
            small,
            small,
            small,
            pltpu.VMEM((1, TOK, KW), BF16),
            small,
            pltpu.VMEM((ROWS, KW), F32),
        ),
        in_specs=[
            in_hbm,
            in_hbm,
            pl.BlockSpec(memory_space=pltpu.VMEM),
            in_hbm,
            in_hbm,
            in_hbm,
            in_hbm,
            in_hbm,
            in_hbm,
            in_hbm,
        ],
        out_specs=(pl.BlockSpec(memory_space=pltpu.VMEM),) * 6,
        scratch_shapes=scratch,
        name="step",
        compiler_params=pltpu.CompilerParams(
            collective_id=0, has_side_effects=True, vmem_limit_bytes=55 * 2**20
        ),
    )(
        tokens, key_cot, norm_gain.reshape(16, 128), key_weight, first_moment, second_moment, inner_step,
        global_prev, outer_momentum, replica_prev,
    )
    return pl.pallas_call(
        hand_over,
        out_shape=tuple(jax.ShapeDtypeStruct(a.shape, a.dtype) for a in results),
        in_specs=[pl.BlockSpec(memory_space=pltpu.VMEM)] * 6,
        out_specs=(pl.BlockSpec(memory_space=pltpu.HBM),) * 6,
        scratch_shapes=[pltpu.SemaphoreType.DMA((6,))],
        name="hand_over",
        compiler_params=pltpu.CompilerParams(vmem_limit_bytes=4 * 2**20),
    )(*results)


def solution(mesh):
    split = P("replica", "fsdp", None)
    rows = P("fsdp", None)
    return jax.shard_map(
        body,
        mesh=mesh,
        in_specs=(split, split, P(), split, split, split, P(), rows, rows, split),
        out_specs=(split, split, split, split, split, rows),
        check_vma=False,
    )
```

```python
import math

import jax
import jax.numpy as jnp
from jax import lax
from jax.experimental import pallas as pl
from jax.experimental.pallas import tpu as pltpu
from jax.sharding import PartitionSpec as P

F32, BF16 = jnp.float32, jnp.bfloat16
MESH = pl.DeviceIdType.MESH
TOK, D, KW, ROWS, WIDE = 512, 2048, 512, 64, 256
CONTRACT_FIRST = (((0,), (0,)), ((), ()))

CHUNKS = (
    (1, 32, 16, "x"),
    (1, 0, 16, "x"),
    (1, 48, 16, "z"),
    (1, 16, 16, "x"),
    (0, 0, 16, "z"),
    (0, 16, 16, "x"),
    (0, 32, 16, "x"),
    (0, 48, 16, "x"),
)
HALVES = (1, 0)
OFFSETS = (2, 1, 3)


class Place:
    def __init__(self):
        f, r = lax.axis_index("fsdp"), lax.axis_index("replica")
        self.x, self.z, self.c = f // 8, (f // 2) % 4, f % 2
        self.y, self.l = r // 2, r % 2

    def at(self, **other):
        v = {**vars(self), **other}
        return (v["y"] * 2 + v["l"], (v["x"] * 4 + v["z"]) * 2 + v["c"])

    def partners(self):
        for o in OFFSETS:
            yield self.at(z=(self.z + o) % 4)
        for o in OFFSETS:
            yield self.at(x=(self.x + o) % 4)
        yield self.at(c=1 - self.c)
        yield self.at(l=1 - self.l)
        yield self.at(y=(self.y + 1) % 8)
        yield self.at(y=(self.y + 7) % 8)


def up(ref_value):
    return ref_value.astype(F32)


def remote(src, dst, send_sem, recv_sem, to):
    return pltpu.make_async_remote_copy(
        src_ref=src,
        dst_ref=dst,
        send_sem=send_sem,
        recv_sem=recv_sem,
        device_id=to,
        device_id_type=MESH,
    )


def chunk_steps(here, chunk, bufs, sems, w_ref, adam):
    half, row0, nr, axis = chunk
    g, rc, s1, r1, sq, rq = bufs
    send_sem, recv_sem = sems
    other_axis = "z" if axis == "x" else "x"
    p, q, c = getattr(here, axis), getattr(here, other_axis), here.c
    sibling = here.at(c=1 - c)

    def along_p(o):
        return here.at(**{axis: (p + o) % 4})

    def along_q(o):
        return here.at(**{other_axis: (q + o) % 4})

    def send(n, src, dst, to, m=None):
        one = remote(src, dst, send_sem.at[n], recv_sem.at[n if m is None else m], to)
        one.start()
        return one

    def all_of(n, ref):
        return remote(ref, ref, send_sem.at[n], recv_sem.at[n], sibling)

    swap = send(0, g.at[1 - c], rc, sibling)
    yield
    swap.wait_recv()
    for o in OFFSETS:
        to = (p + o) % 4
        s1[to] = (up(g[c, to]) + up(rc[to])).astype(BF16)
        send(1, s1.at[to], r1.at[o - 1], along_p(o))
    yield
    mine = up(g[c, p]) + up(rc[p])
    all_of(1, r1).wait_recv()
    sq[...] = (mine + up(r1[0]) + up(r1[1]) + up(r1[2])).astype(BF16)
    for o in OFFSETS:
        send(2, sq.at[(q + o) % 4], rq.at[o - 1], along_q(o))
    yield
    swap.wait_send()
    all_of(2, rq).wait_recv()
    w_own = adam(half, row0, nr, up(sq[q]) + up(rq[0]) + up(rq[1]) + up(rq[2]))

    def piece(pp, qq, cc):
        x, z = (pp, qq) if axis == "x" else (qq, pp)
        return w_ref.at[half, x, z, cc, pl.ds(row0, nr)]

    def group(pp, cc):
        if axis == "x":
            return w_ref.at[half, pp, :, cc, pl.ds(row0, nr)]
        return w_ref.at[half, :, pp, cc, pl.ds(row0, nr)]

    own = piece(p, q, c)
    own[...] = w_own
    for o in OFFSETS:
        send(3, own, own, along_q(o))
    yield
    all_of(1, r1).wait_send()
    all_of(3, rq).wait_recv()
    own = group(p, c)
    come = [send(4, own, own, along_p(o), 4 + o) for o in OFFSETS]
    send(8, own, own, sibling)
    yield
    all_of(2, rq).wait_send()
    all_of(3, rq).wait_send()
    for i, o in ((1, 1), (2, 3), (0, 2)):
        come[i].wait_recv()
        got = group((p + 4 - o) % 4, c)
        send(8, got, got, sibling)
    yield
    all_of(4, r1).wait_send()
    all_of(8, s1).wait()
    yield


def kernel(
    tokens, key_cot, gain, key_weight, first_moment, second_moment, inner_step, global_prev, outer_momentum, replica_prev,
    weight_out, first_out, second_out, keys_out, blended_out, momentum_out,
    tok, cot, cs, scale, kw, m1, m2, gp, om, rp, gcol, w_all, ds, dy,
    step_smem, in_sem, d_send, d_recv, *chunk_scratch,
):
    here = Place()
    c = here.c

    def load(src, dst, n):
        one = pltpu.make_async_copy(src, dst, in_sem.at[n])
        one.start()
        return one

    quarter = TOK // 4
    tok_in = [load(tokens.at[0, pl.ds(i * quarter, quarter)], tok.at[pl.ds(i * quarter, quarter)], i) for i in range(4)]
    cot_in = load(key_cot.at[0], cot, 4)
    barrier = pltpu.get_barrier_semaphore()
    n_partners = 0
    for to in here.partners():
        pl.semaphore_signal(barrier, inc=1, device_id=to, device_id_type=MESH)
        n_partners += 1

    rest = [
        load(key_weight.at[0], kw, 5),
        load(first_moment.at[0], m1, 6),
        load(second_moment.at[0], m2, 7),
        load(global_prev, gp, 8),
        load(outer_momentum, om, 9),
        load(inner_step, step_smem, 11),
    ]
    rp_in = load(replica_prev.at[0], rp, 10)

    for i in range(4):
        tok_in[i].wait()
        if i == 0:
            cot_in.wait()
        rows = slice(i * quarter, (i + 1) * quarter)
        v = up(tok[rows, :])
        s = lax.rsqrt(jnp.sum(v * v, axis=1, keepdims=True) * (1.0 / D) + 1e-05)
        scale[rows, :] = s
        cs[rows, :] = (up(cot[rows, :]) * s).astype(BF16)

    def gemm1(half):
        for x in range(4):
            part = lax.dot_general(
                tok[:, x * 512 : (x + 1) * 512],
                cs[:, half * WIDE : (half + 1) * WIDE],
                CONTRACT_FIRST,
                preferred_element_type=F32,
            ).astype(BF16)
            for i, (h, row0, nr, axis) in enumerate(CHUNKS):
                if h != half:
                    continue
                g = chunk_scratch[8 * i]
                for z in range(4):
                    p, q = (x, z) if axis == "x" else (z, x)
                    for cc in range(2):
                        at = (z * 2 + cc) * ROWS + row0
                        g[cc, p, q] = part[at : at + nr]

    def adam(half, row0, nr, total):
        rows, cols = slice(row0, row0 + nr), slice(half * WIDE, (half + 1) * WIDE)
        count = jnp.full((1, WIDE), step_smem[0], jnp.int32).astype(F32)
        gains = gcol[rows, :]
        grads = total * gains
        first_new = 0.9 * m1[rows, cols] + 0.1 * grads
        second_new = 0.95 * m2[rows, cols] + 0.05 * grads * grads
        first_hat = first_new / (1.0 - jnp.exp(count * math.log(0.9)))
        second_hat = second_new / (1.0 - jnp.exp(count * math.log(0.95)))
        weight = kw[rows, cols]
        change = 0.03 * (first_hat / (jnp.sqrt(second_hat) + 1e-08) + 0.1 * weight)
        weight_new = weight - change
        first_out[0, rows, cols] = first_new
        second_out[0, rows, cols] = second_new
        weight_out[0, rows, cols] = weight_new
        return (weight_new * gains).astype(BF16)

    def drift_steps():
        y = here.y
        rp_in.wait()
        ds[0] = rp[...].astype(BF16)
        swap = remote(ds.at[0], ds.at[1], d_send.at[0], d_recv.at[0], here.at(l=1 - here.l))
        swap.start()
        yield
        swap.wait()
        dy[y] = (up(ds[0]) + up(ds[1])).astype(BF16)
        went = []
        for k in range(4):
            come = []
            for n, step in ((1 + k, 1), (5 + k, 7)):
                if k == 3 and step == 7:
                    continue
                slot = dy.at[(y + (8 - step) * k) % 8]
                one = remote(slot, slot, d_send.at[n], d_recv.at[n], here.at(y=(y + step) % 8))
                one.start()
                come.append(one)
            went += come
            yield
            for one in come:
                one.wait_recv()
        total = up(dy[0])
        for i in range(1, 8):
            total = total + up(dy[i])
        mean_drift = gp[...] - total * (1.0 / 16)
        momentum_new = 0.9 * om[...] + mean_drift
        global_new = gp[...] - 0.7 * (mean_drift + 0.9 * momentum_new)
        momentum_out[...] = momentum_new
        blended_out[0] = 0.5 * global_new + 0.5 * rp[...]
        for one in went:
            one.wait_send()
        yield

    def gemm2(half):
        w = w_all[half].reshape(D, WIDE)
        cols = slice(half * WIDE, (half + 1) * WIDE)
        part = jnp.dot(tok[...], w, preferred_element_type=F32)
        keys_out[0, :, cols] = (part * scale[...]).astype(BF16)

    chunks = [
        chunk_steps(here, chunk, chunk_scratch[8 * i : 8 * i + 6], chunk_scratch[8 * i + 6 : 8 * i + 8], w_all, adam)
        for i, chunk in enumerate(CHUNKS)
    ]
    drift = drift_steps()

    gemm1(HALVES[0])
    pl.semaphore_wait(barrier, n_partners)
    for i, chunk in enumerate(CHUNKS):
        if chunk[0] == HALVES[0]:
            next(chunks[i])
    next(drift)
    gemm1(HALVES[1])
    for i, chunk in enumerate(CHUNKS):
        if chunk[0] == HALVES[1]:
            next(chunks[i])
    for one in rest:
        one.wait()
    lane = lax.broadcasted_iota(jnp.int32, (ROWS, 128), 1)
    row = lax.broadcasted_iota(jnp.int32, (ROWS, 128), 0)
    gains = gain[pl.ds(here.x * 4 + here.z, 1), :]
    picked = jnp.where(lane == row + ROWS * c, jnp.broadcast_to(gains, (ROWS, 128)), 0.0)
    gcol[...] = jnp.broadcast_to(jnp.sum(picked, axis=1, keepdims=True), (ROWS, WIDE))

    for level in range(1, 6):
        for one in chunks:
            next(one)
        next(drift)
    for half in HALVES:
        for i, chunk in enumerate(CHUNKS):
            if chunk[0] == half:
                next(chunks[i])
        gemm2(half)


def chunk_scratch(nr):
    return [
        pltpu.VMEM((2, 4, 4, nr, WIDE), BF16),
        pltpu.VMEM((4, 4, nr, WIDE), BF16),
        pltpu.VMEM((4, 4, nr, WIDE), BF16),
        pltpu.VMEM((3, 4, nr, WIDE), BF16),
        pltpu.VMEM((4, nr, WIDE), BF16),
        pltpu.VMEM((3, nr, WIDE), BF16),
        pltpu.SemaphoreType.DMA((9,)),
        pltpu.SemaphoreType.DMA((9,)),
    ]


def hand_over(*refs):
    sems = refs[12]
    copies = [pltpu.make_async_copy(refs[i], refs[6 + i], sems.at[i]) for i in range(6)]
    for one in copies:
        one.start()
    for one in copies:
        one.wait()


def body(tokens, key_cot, norm_gain, key_weight, first_moment, second_moment, inner_step, global_prev, outer_momentum, replica_prev):
    anywhere = pl.BlockSpec(memory_space=pl.ANY)
    in_hbm = pl.BlockSpec(memory_space=pltpu.HBM)
    small = pltpu.VMEM((1, ROWS, KW), F32)
    shard = pltpu.VMEM((ROWS, KW), F32)
    scratch = [
        pltpu.VMEM((TOK, D), BF16),
        pltpu.VMEM((TOK, KW), BF16),
        pltpu.VMEM((TOK, KW), BF16),
        pltpu.VMEM((TOK, 1), F32),
        *[shard] * 6,
        pltpu.VMEM((ROWS, WIDE), F32),
        pltpu.VMEM((2, 4, 4, 2, ROWS, WIDE), BF16),
        pltpu.VMEM((2, ROWS, KW), BF16),
        pltpu.VMEM((8, ROWS, KW), BF16),
        pltpu.SMEM((1,), jnp.int32),
        pltpu.SemaphoreType.DMA((12,)),
        pltpu.SemaphoreType.DMA((8,)),
        pltpu.SemaphoreType.DMA((8,)),
    ]
    for chunk in CHUNKS:
        scratch += chunk_scratch(chunk[2])
    results = pl.pallas_call(
        kernel,
        out_shape=(
            small,
            small,
            small,
            pltpu.VMEM((1, TOK, KW), BF16),
            small,
            pltpu.VMEM((ROWS, KW), F32),
        ),
        in_specs=[
            in_hbm,
            in_hbm,
            pl.BlockSpec(memory_space=pltpu.VMEM),
            in_hbm,
            in_hbm,
            in_hbm,
            in_hbm,
            in_hbm,
            in_hbm,
            in_hbm,
        ],
        out_specs=(pl.BlockSpec(memory_space=pltpu.VMEM),) * 6,
        scratch_shapes=scratch,
        name="step",
        compiler_params=pltpu.CompilerParams(
            collective_id=0, has_side_effects=True, vmem_limit_bytes=55 * 2**20
        ),
    )(
        tokens, key_cot, norm_gain.reshape(16, 128), key_weight, first_moment, second_moment, inner_step,
        global_prev, outer_momentum, replica_prev,
    )
    return pl.pallas_call(
        hand_over,
        out_shape=tuple(jax.ShapeDtypeStruct(a.shape, a.dtype) for a in results),
        in_specs=[pl.BlockSpec(memory_space=pltpu.VMEM)] * 6,
        out_specs=(pl.BlockSpec(memory_space=pltpu.HBM),) * 6,
        scratch_shapes=[pltpu.SemaphoreType.DMA((6,))],
        name="hand_over",
        compiler_params=pltpu.CompilerParams(vmem_limit_bytes=4 * 2**20),
    )(*results)


def solution(mesh):
    split = P("replica", "fsdp", None)
    rows = P("fsdp", None)
    return jax.shard_map(
        body,
        mesh=mesh,
        in_specs=(split, split, P(), split, split, split, P(), rows, rows, split),
        out_specs=(split, split, split, split, split, rows),
        check_vma=False,
    )
```

```python
import math

import jax
import jax.numpy as jnp
from jax import lax
from jax.experimental import pallas as pl
from jax.experimental.pallas import tpu as pltpu
from jax.sharding import PartitionSpec as P

F32, BF16 = jnp.float32, jnp.bfloat16
MESH = pl.DeviceIdType.MESH
TOK, D, KW, ROWS, WIDE = 512, 2048, 512, 64, 256
CONTRACT_FIRST = (((0,), (0,)), ((), ()))

CHUNKS = (
    (1, 32, 16, "x"),
    (1, 0, 16, "x"),
    (1, 48, 16, "z"),
    (1, 16, 16, "x"),
    (0, 0, 16, "z"),
    (0, 16, 16, "x"),
    (0, 32, 16, "x"),
    (0, 48, 16, "x"),
)
HALVES = (1, 0)
OFFSETS = (2, 1, 3)


class Place:
    def __init__(self):
        f, r = lax.axis_index("fsdp"), lax.axis_index("replica")
        self.x, self.z, self.c = f // 8, (f // 2) % 4, f % 2
        self.y, self.l = r // 2, r % 2

    def at(self, **other):
        v = {**vars(self), **other}
        return (v["y"] * 2 + v["l"], (v["x"] * 4 + v["z"]) * 2 + v["c"])

    def partners(self):
        for o in OFFSETS:
            yield self.at(z=(self.z + o) % 4)
        for o in OFFSETS:
            yield self.at(x=(self.x + o) % 4)
        yield self.at(c=1 - self.c)
        yield self.at(l=1 - self.l)
        yield self.at(y=(self.y + 1) % 8)
        yield self.at(y=(self.y + 7) % 8)


def up(ref_value):
    return ref_value.astype(F32)


def remote(src, dst, send_sem, recv_sem, to):
    return pltpu.make_async_remote_copy(
        src_ref=src,
        dst_ref=dst,
        send_sem=send_sem,
        recv_sem=recv_sem,
        device_id=to,
        device_id_type=MESH,
    )


def chunk_steps(here, chunk, bufs, sems, w_ref, adam):
    half, row0, nr, axis = chunk
    offsets = OFFSETS if row0 % 32 == 0 else (2, 3, 1)
    g, rc, s1, r1, sq, rq = bufs
    send_sem, recv_sem = sems
    other_axis = "z" if axis == "x" else "x"
    p, q, c = getattr(here, axis), getattr(here, other_axis), here.c
    sibling = here.at(c=1 - c)

    def along_p(o):
        return here.at(**{axis: (p + o) % 4})

    def along_q(o):
        return here.at(**{other_axis: (q + o) % 4})

    def send(n, src, dst, to, m=None):
        one = remote(src, dst, send_sem.at[n], recv_sem.at[n if m is None else m], to)
        one.start()
        return one

    def all_of(n, ref):
        return remote(ref, ref, send_sem.at[n], recv_sem.at[n], sibling)

    swap = send(0, g.at[1 - c], rc, sibling)
    yield
    swap.wait_recv()
    for o in offsets:
        to = (p + o) % 4
        s1[to] = (up(g[c, to]) + up(rc[to])).astype(BF16)
        send(1, s1.at[to], r1.at[o - 1], along_p(o))
    yield
    mine = up(g[c, p]) + up(rc[p])
    all_of(1, r1).wait_recv()
    sq[...] = (mine + up(r1[0]) + up(r1[1]) + up(r1[2])).astype(BF16)
    for o in offsets:
        send(2, sq.at[(q + o) % 4], rq.at[o - 1], along_q(o))
    yield
    swap.wait_send()
    all_of(2, rq).wait_recv()
    w_own = adam(half, row0, nr, up(sq[q]) + up(rq[0]) + up(rq[1]) + up(rq[2]))

    def piece(pp, qq, cc):
        x, z = (pp, qq) if axis == "x" else (qq, pp)
        return w_ref.at[half, x, z, cc, pl.ds(row0, nr)]

    def group(pp, cc):
        if axis == "x":
            return w_ref.at[half, pp, :, cc, pl.ds(row0, nr)]
        return w_ref.at[half, :, pp, cc, pl.ds(row0, nr)]

    own = piece(p, q, c)
    own[...] = w_own
    for o in offsets:
        send(3, own, own, along_q(o))
    yield
    all_of(1, r1).wait_send()
    all_of(3, rq).wait_recv()
    own = group(p, c)
    come = [send(4, own, own, along_p(o), 4 + o) for o in offsets]
    send(8, own, own, sibling)
    yield
    all_of(2, rq).wait_send()
    all_of(3, rq).wait_send()
    for o in (1, 3, 2):
        come[offsets.index(o)].wait_recv()
        got = group((p + 4 - o) % 4, c)
        send(8, got, got, sibling)
    yield
    all_of(4, r1).wait_send()
    all_of(8, s1).wait()
    yield


def kernel(
    tokens, key_cot, gain, key_weight, first_moment, second_moment, inner_step, global_prev, outer_momentum, replica_prev,
    weight_out, first_out, second_out, keys_out, blended_out, momentum_out,
    tok, cot, cs, scale, kw, m1, m2, gp, om, rp, gcol, w_all, ds, dy,
    step_smem, in_sem, d_send, d_recv, *chunk_scratch,
):
    here = Place()
    c = here.c

    def load(src, dst, n):
        one = pltpu.make_async_copy(src, dst, in_sem.at[n])
        one.start()
        return one

    quarter = TOK // 4
    tok_in = [load(tokens.at[0, pl.ds(i * quarter, quarter)], tok.at[pl.ds(i * quarter, quarter)], i) for i in range(4)]
    cot_in = load(key_cot.at[0], cot, 4)
    barrier = pltpu.get_barrier_semaphore()
    n_partners = 0
    for to in here.partners():
        pl.semaphore_signal(barrier, inc=1, device_id=to, device_id_type=MESH)
        n_partners += 1

    rest = [
        load(key_weight.at[0], kw, 5),
        load(first_moment.at[0], m1, 6),
        load(second_moment.at[0], m2, 7),
        load(global_prev, gp, 8),
        load(outer_momentum, om, 9),
        load(inner_step, step_smem, 11),
    ]
    rp_in = load(replica_prev.at[0], rp, 10)

    for i in range(4):
        tok_in[i].wait()
        if i == 0:
            cot_in.wait()
        rows = slice(i * quarter, (i + 1) * quarter)
        v = up(tok[rows, :])
        s = lax.rsqrt(jnp.sum(v * v, axis=1, keepdims=True) * (1.0 / D) + 1e-05)
        scale[rows, :] = s
        cs[rows, :] = (up(cot[rows, :]) * s).astype(BF16)

    def gemm1(half):
        for x in range(4):
            part = lax.dot_general(
                tok[:, x * 512 : (x + 1) * 512],
                cs[:, half * WIDE : (half + 1) * WIDE],
                CONTRACT_FIRST,
                preferred_element_type=F32,
            ).astype(BF16)
            for i, (h, row0, nr, axis) in enumerate(CHUNKS):
                if h != half:
                    continue
                g = chunk_scratch[8 * i]
                for z in range(4):
                    p, q = (x, z) if axis == "x" else (z, x)
                    for cc in range(2):
                        at = (z * 2 + cc) * ROWS + row0
                        g[cc, p, q] = part[at : at + nr]

    def adam(half, row0, nr, total):
        rows, cols = slice(row0, row0 + nr), slice(half * WIDE, (half + 1) * WIDE)
        count = jnp.full((1, WIDE), step_smem[0], jnp.int32).astype(F32)
        gains = gcol[rows, :]
        grads = total * gains
        first_new = 0.9 * m1[rows, cols] + 0.1 * grads
        second_new = 0.95 * m2[rows, cols] + 0.05 * grads * grads
        first_hat = first_new / (1.0 - jnp.exp(count * math.log(0.9)))
        second_hat = second_new / (1.0 - jnp.exp(count * math.log(0.95)))
        weight = kw[rows, cols]
        change = 0.03 * (first_hat / (jnp.sqrt(second_hat) + 1e-08) + 0.1 * weight)
        weight_new = weight - change
        first_out[0, rows, cols] = first_new
        second_out[0, rows, cols] = second_new
        weight_out[0, rows, cols] = weight_new
        return (weight_new * gains).astype(BF16)

    def drift_steps():
        y = here.y
        rp_in.wait()
        ds[0] = rp[...].astype(BF16)
        swap = remote(ds.at[0], ds.at[1], d_send.at[0], d_recv.at[0], here.at(l=1 - here.l))
        swap.start()
        yield
        swap.wait()
        dy[y] = (up(ds[0]) + up(ds[1])).astype(BF16)
        went = []
        for k in range(4):
            come = []
            for n, step in ((1 + k, 1), (5 + k, 7)):
                if k == 3 and step == 7:
                    continue
                slot = dy.at[(y + (8 - step) * k) % 8]
                one = remote(slot, slot, d_send.at[n], d_recv.at[n], here.at(y=(y + step) % 8))
                one.start()
                come.append(one)
            went += come
            yield
            for one in come:
                one.wait_recv()
        total = up(dy[0])
        for i in range(1, 8):
            total = total + up(dy[i])
        mean_drift = gp[...] - total * (1.0 / 16)
        momentum_new = 0.9 * om[...] + mean_drift
        global_new = gp[...] - 0.7 * (mean_drift + 0.9 * momentum_new)
        momentum_out[...] = momentum_new
        blended_out[0] = 0.5 * global_new + 0.5 * rp[...]
        for one in went:
            one.wait_send()
        yield

    def gemm2(half):
        w = w_all[half].reshape(D, WIDE)
        cols = slice(half * WIDE, (half + 1) * WIDE)
        part = jnp.dot(tok[...], w, preferred_element_type=F32)
        keys_out[0, :, cols] = (part * scale[...]).astype(BF16)

    chunks = [
        chunk_steps(here, chunk, chunk_scratch[8 * i : 8 * i + 6], chunk_scratch[8 * i + 6 : 8 * i + 8], w_all, adam)
        for i, chunk in enumerate(CHUNKS)
    ]
    drift = drift_steps()

    gemm1(HALVES[0])
    pl.semaphore_wait(barrier, n_partners)
    for i, chunk in enumerate(CHUNKS):
        if chunk[0] == HALVES[0]:
            next(chunks[i])
    next(drift)
    gemm1(HALVES[1])
    for i, chunk in enumerate(CHUNKS):
        if chunk[0] == HALVES[1]:
            next(chunks[i])
    for one in rest:
        one.wait()
    lane = lax.broadcasted_iota(jnp.int32, (ROWS, 128), 1)
    row = lax.broadcasted_iota(jnp.int32, (ROWS, 128), 0)
    gains = gain[pl.ds(here.x * 4 + here.z, 1), :]
    picked = jnp.where(lane == row + ROWS * c, jnp.broadcast_to(gains, (ROWS, 128)), 0.0)
    gcol[...] = jnp.broadcast_to(jnp.sum(picked, axis=1, keepdims=True), (ROWS, WIDE))

    for level in range(1, 6):
        for one in chunks:
            next(one)
        next(drift)
    for half in HALVES:
        for i, chunk in enumerate(CHUNKS):
            if chunk[0] == half:
                next(chunks[i])
        gemm2(half)


def chunk_scratch(nr):
    return [
        pltpu.VMEM((2, 4, 4, nr, WIDE), BF16),
        pltpu.VMEM((4, 4, nr, WIDE), BF16),
        pltpu.VMEM((4, 4, nr, WIDE), BF16),
        pltpu.VMEM((3, 4, nr, WIDE), BF16),
        pltpu.VMEM((4, nr, WIDE), BF16),
        pltpu.VMEM((3, nr, WIDE), BF16),
        pltpu.SemaphoreType.DMA((9,)),
        pltpu.SemaphoreType.DMA((9,)),
    ]


def hand_over(*refs):
    sems = refs[12]
    copies = [pltpu.make_async_copy(refs[i], refs[6 + i], sems.at[i]) for i in range(6)]
    for one in copies:
        one.start()
    for one in copies:
        one.wait()


def body(tokens, key_cot, norm_gain, key_weight, first_moment, second_moment, inner_step, global_prev, outer_momentum, replica_prev):
    anywhere = pl.BlockSpec(memory_space=pl.ANY)
    in_hbm = pl.BlockSpec(memory_space=pltpu.HBM)
    small = pltpu.VMEM((1, ROWS, KW), F32)
    shard = pltpu.VMEM((ROWS, KW), F32)
    scratch = [
        pltpu.VMEM((TOK, D), BF16),
        pltpu.VMEM((TOK, KW), BF16),
        pltpu.VMEM((TOK, KW), BF16),
        pltpu.VMEM((TOK, 1), F32),
        *[shard] * 6,
        pltpu.VMEM((ROWS, WIDE), F32),
        pltpu.VMEM((2, 4, 4, 2, ROWS, WIDE), BF16),
        pltpu.VMEM((2, ROWS, KW), BF16),
        pltpu.VMEM((8, ROWS, KW), BF16),
        pltpu.SMEM((1,), jnp.int32),
        pltpu.SemaphoreType.DMA((12,)),
        pltpu.SemaphoreType.DMA((8,)),
        pltpu.SemaphoreType.DMA((8,)),
    ]
    for chunk in CHUNKS:
        scratch += chunk_scratch(chunk[2])
    results = pl.pallas_call(
        kernel,
        out_shape=(
            small,
            small,
            small,
            pltpu.VMEM((1, TOK, KW), BF16),
            small,
            pltpu.VMEM((ROWS, KW), F32),
        ),
        in_specs=[
            in_hbm,
            in_hbm,
            pl.BlockSpec(memory_space=pltpu.VMEM),
            in_hbm,
            in_hbm,
            in_hbm,
            in_hbm,
            in_hbm,
            in_hbm,
            in_hbm,
        ],
        out_specs=(pl.BlockSpec(memory_space=pltpu.VMEM),) * 6,
        scratch_shapes=scratch,
        name="step",
        compiler_params=pltpu.CompilerParams(
            collective_id=0, has_side_effects=True, vmem_limit_bytes=55 * 2**20
        ),
    )(
        tokens, key_cot, norm_gain.reshape(16, 128), key_weight, first_moment, second_moment, inner_step,
        global_prev, outer_momentum, replica_prev,
    )
    return pl.pallas_call(
        hand_over,
        out_shape=tuple(jax.ShapeDtypeStruct(a.shape, a.dtype) for a in results),
        in_specs=[pl.BlockSpec(memory_space=pltpu.VMEM)] * 6,
        out_specs=(pl.BlockSpec(memory_space=pltpu.HBM),) * 6,
        scratch_shapes=[pltpu.SemaphoreType.DMA((6,))],
        name="hand_over",
        compiler_params=pltpu.CompilerParams(vmem_limit_bytes=4 * 2**20),
    )(*results)


def solution(mesh):
    split = P("replica", "fsdp", None)
    rows = P("fsdp", None)
    return jax.shard_map(
        body,
        mesh=mesh,
        in_specs=(split, split, P(), split, split, split, P(), rows, rows, split),
        out_specs=(split, split, split, split, split, rows),
        check_vma=False,
    )
```
